128 devices in a mesh: grp: 8 (over x, core), sp: 16 (over z, y).
Axes of the slice: x: 4, y: 4, z: 4, core: 2. Of those that a mesh axis runs over, the one named last changes fastest.
Arguments:
- qkv: bfloat16 [64, 1024, 3, 2048], P('grp', 'sp'), may hold values from -6 to 6
- tokens: bfloat16 [64, 1024, 3072], P('grp', 'sp'), may hold values from -3 to 3
- lengths: int32 [64], replicated, may hold values from 1 to 1024, as said below
- t_index: int32 [64], replicated, may hold values from 0 to 49
- slot_target: int32 [64], replicated, may hold values from 0 to 63, as said below
- gate_table: float32 [50, 3072], replicated, may hold values from -12 to 12
- q_gain: float32 [128], replicated, may hold values from 0.1 to 1.9
- k_gain: float32 [128], replicated, may hold values from 0.1 to 1.9
- out_weight: bfloat16 [2048, 3072], replicated, may hold values from -0.5 to 0.5
Outputs:
- mixed: bfloat16 [64, 1024, 3072], P('grp', 'sp')
The draws below stay inside these ranges and needn't reach their ends.
Inputs may be any that keep to these rules, and one draw needn't show every extreme that they name: Token positions from lengths[c] on are padding of clip c; some clip has exactly 1024 live tokens. `slot_target`: A permutation of the 64 clip slots; slots g * 8 to (g + 1) * 8 - 1 belong to group g, and clips g * 8 to (g + 1) * 8 - 1 start in group g. Every group sends exactly 1 of its clips to each group, itself included.
All inputs are finite; a program needn't handle non-finite values.
Results may differ from the reference program's by a relative error of at most 0.0065.
Values may be sent and summed in bfloat16 or wider, within the bound.
No kernel may reach another device: no remote copies, remote signals or barrier semaphores. Data moves between devices by JAX's collectives and lax.ppermute only.
A program may use at most 128 MiB of HBM per device.

```python
import jax
import jax.numpy as jnp
from jax import lax

D = 3072
HEADS = 16
HD = 128
STEPS = 50
LMAX = 1024
CG = 8
CLIPS = 64
N_GRP = 8


def draw_lengths(key, part):
    key = jax.random.fold_in(key, 11)
    key_rank, key_cut = jax.random.split(key)
    ranking = jax.random.permutation(key_rank, N_GRP).astype(jnp.int32)
    low_len = LMAX // 4
    base_len = low_len + (LMAX - low_len) * ranking // (N_GRP - 1)
    cutting = jax.random.randint(key_cut, (N_GRP, CG), 0, LMAX // 8 + 1).astype(jnp.int32)
    result = base_len[:, None] - cutting
    first = jnp.arange(CG, dtype=jnp.int32)[None, :] == 0
    heavy = ranking[:, None] == N_GRP - 1
    result = jnp.where(first & heavy, LMAX, result)
    return jnp.clip(result, 1, LMAX).reshape(-1).astype(jnp.int32)


def draw_slot_target(key, part):
    key = jax.random.fold_in(key, 7)
    key_rank, key_place = jax.random.split(key)
    per_peer = CG // N_GRP
    ranking = jax.vmap(lambda subkey: jax.random.permutation(subkey, CG))(jax.random.split(key_rank, N_GRP))
    placing = jax.vmap(lambda subkey: jax.random.permutation(subkey, CG))(jax.random.split(key_place, N_GRP))
    source = jnp.arange(N_GRP, dtype=jnp.int32)[:, None]
    destination = ranking // per_peer
    within = ranking % per_peer
    position = placing[destination, source * per_peer + within]
    return (destination * CG + position).reshape(-1).astype(jnp.int32)


def plant(values, rng, smallest, largest):
    extent = values.shape
    spot = [jax.random.randint(jax.random.fold_in(rng, axis), (), 0, extent[axis]) for axis in range(len(extent))]
    values = values.at[tuple(spot)].set(smallest)
    longest = extent.index(max(extent))
    spot[longest] = (spot[longest] + 1) % extent[longest]
    return values.at[tuple(spot)].set(largest)


def shard_levels(own_key, extent, shards, low, high):
    def one(axis_at, parts):
        heights = jax.random.uniform(jax.random.fold_in(jax.random.fold_in(own_key, 6), axis_at), (parts,), jnp.float32, low / len(shards), high / len(shards))
        return jnp.repeat(jnp.exp(heights), extent[axis_at] // parts).reshape((-1,) + (1,) * (len(extent) - axis_at - 1))

    level = one(*shards[0])
    for cut in shards[1:]:
        level = level * one(*cut)
    return level


def normal_values(rng, extent, width, most, cuts=(), kind=jnp.bfloat16):
    entries = width * jax.random.normal(rng, extent, jnp.float32)
    if cuts:
        entries = entries * shard_levels(rng, extent, cuts, -0.22, 0.18)
    return jnp.clip(entries, -most, most).astype(kind)


def setup_inputs(seed: int = 0) -> dict:
    streams_of = jax.random.split(jax.random.key(seed), 10)
    return {
        "qkv": normal_values(streams_of[0], (CLIPS, LMAX, 3, HEADS * HD), 1.0, 6.0, ((0, 8), (1, 16))),
        "tokens": normal_values(streams_of[1], (CLIPS, LMAX, D), 0.5, 3.0, ((0, 8), (1, 16))),
        "lengths": draw_lengths(jax.random.fold_in(streams_of[9], 71), 0),
        "t_index": plant(jax.random.randint(streams_of[3], (CLIPS,), 0, STEPS), jax.random.fold_in(streams_of[3], 1), 0, STEPS - 1).astype(jnp.int32),
        "slot_target": draw_slot_target(jax.random.fold_in(streams_of[9], 71), 0),
        "gate_table": normal_values(streams_of[5], (STEPS, D), 2.0, 12.0, (), jnp.float32),
        "q_gain": jnp.clip(1.0 + 0.18 * jax.random.normal(streams_of[6], (HD,), jnp.float32), 0.1, 1.9),
        "k_gain": jnp.clip(1.0 + 0.18 * jax.random.normal(streams_of[7], (HD,), jnp.float32), 0.1, 1.9),
        "out_weight": normal_values(streams_of[8], (HEADS * HD, D), HD ** -0.5, 0.5),
    }


def rms_scale(part, gain):
    wide = part.astype(jnp.float32)
    normed = wide * lax.rsqrt(lax.optimization_barrier(jnp.mean(wide * wide, axis=-1, keepdims=True)) + 1e-06) * gain
    return normed.astype(jnp.bfloat16)

def reference(qkv, tokens, lengths, t_index, slot_target, gate_table, q_gain, k_gain, out_weight):

    def one_clip(item):
        block, resid, length, step_index = item
        shaped = block.reshape(LMAX, 3, HEADS, HD)
        queries = lax.optimization_barrier(rms_scale(shaped[:, 0], q_gain)).astype(jnp.float32)
        key_rows = lax.optimization_barrier(rms_scale(shaped[:, 1], k_gain)).astype(jnp.float32)
        value_rows = shaped[:, 2].astype(jnp.float32)
        scores = jnp.einsum('qhd,khd->hqk', queries, key_rows) * HD ** (-0.5)
        key_live = jnp.arange(LMAX, dtype=jnp.int32) < length
        raised = jnp.where(key_live[None, None, :], jnp.exp(scores), jnp.float32(0.0))
        weights = (raised / lax.optimization_barrier(jnp.sum(raised, axis=-1, keepdims=True))).astype(jnp.bfloat16)
        weights = lax.optimization_barrier(weights).astype(jnp.float32)
        attended = jnp.einsum('hqk,khd->qhd', weights, value_rows)
        attended = jnp.where(key_live[:, None, None], attended, jnp.float32(0.0)).astype(jnp.bfloat16)
        attended = lax.optimization_barrier(attended)
        projected = jnp.dot(attended.reshape(LMAX, HEADS * HD), out_weight, preferred_element_type=jnp.float32)
        gate_row = gate_table[step_index]
        return (resid.astype(jnp.float32) + gate_row[None, :] * projected).astype(jnp.bfloat16)
    results = lax.map(one_clip, (qkv, tokens, lengths, t_index))
    return jnp.zeros_like(results).at[slot_target].set(results)
```

```python
import functools
import math

import jax
import jax.numpy as jnp
from jax import lax
from jax.experimental import pallas as pl
from jax.experimental.pallas import tpu as pltpu
from jax.sharding import PartitionSpec as P

HEADS = 16
HD = 128
CG = 8
TILE = 256
CHUNKS = ((4, 2), (6, 2), (2, 2), (0, 2))
SCALE = math.log2(math.e) / math.sqrt(HD)
VMEM_LIMIT = 24 * 2**20


def params(limit=VMEM_LIMIT):
    return pltpu.CompilerParams(vmem_limit_bytes=limit)


def in_vmem(array):
    return pltpu.with_memory_space_constraint(array, pltpu.VMEM)


def meta_kernel(group_ref, length_ref, step_ref, slot_ref, meta_ref):
    group = group_ref[0]
    for i in range(CG):
        clip = group * CG + i
        k = lax.shift_right_logical(slot_ref[clip], 3) ^ group
        meta_ref[k] = i
        meta_ref[CG + k] = length_ref[clip]
        meta_ref[2 * CG + k] = step_ref[clip]
    for clip in range(slot_ref.shape[0]):
        slot = slot_ref[clip]

        @pl.when(lax.shift_right_logical(slot, 3) == group)
        def _(slot=slot, clip=clip):
            meta_ref[3 * CG + ((clip // CG) ^ group)] = slot & 7


def make_meta(group, lengths, t_index, slot_target):
    smem = pl.BlockSpec(memory_space=pltpu.SMEM)
    return pl.pallas_call(
        meta_kernel,
        out_shape=jax.ShapeDtypeStruct((4 * CG,), jnp.int32),
        in_specs=[smem] * 4,
        out_specs=smem,
        name="meta",
    )(group, lengths, t_index, slot_target)


def prep_kernel(meta_ref, x_ref, o_ref):
    j = pl.program_id(0)
    for h in range(HEADS):
        o_ref[h, j] = x_ref[0, :, :, h * HD : (h + 1) * HD]


def prep(meta, x, first, count):
    rows = x.shape[2]
    return pl.pallas_call(
        prep_kernel,
        grid_spec=pltpu.PrefetchScalarGridSpec(
            num_scalar_prefetch=1,
            grid=(count,),
            in_specs=[
                pl.BlockSpec((1, 3, rows, HEADS * HD), lambda j, m: (m[first + j], 0, 0, 0))
            ],
            out_specs=pl.BlockSpec(memory_space=pltpu.VMEM),
        ),
        out_shape=pltpu.VMEM((HEADS, count, 3, rows, HD), jnp.bfloat16),
        compiler_params=params(),
        name="prep",
    )(meta, x)


def rms(part, gain):
    wide = part.astype(jnp.float32)
    mean = jnp.mean(wide * wide, axis=-1, keepdims=True)
    return (wide * lax.rsqrt(mean + 1e-06) * gain).astype(jnp.bfloat16)


def attention_kernel(first, count, meta_ref, y_ref, qg_ref, kg_ref, o_ref, q_ref, k_ref, v_ref):
    blocks, rows = y_ref.shape[0], y_ref.shape[3]
    total = blocks * rows
    tiles = total // TILE
    per_tile = TILE // rows
    q_gain, k_gain = qg_ref[...], kg_ref[...]

    for c in range(count):
        length = meta_ref[CG + first + c]
        live_tiles = lax.div(length + (TILE - 1), TILE)
        for t in range(tiles):
            at = slice(t * per_tile, (t + 1) * per_tile)
            to = slice(t * TILE, (t + 1) * TILE)

            @pl.when(t < live_tiles)
            def _(at=at, to=to, t=t):
                q_ref[to] = rms(y_ref[at, c, 0].reshape(TILE, HD), q_gain)
                k_ref[to] = rms(y_ref[at, c, 1].reshape(TILE, HD), k_gain)
                row = t * TILE + lax.broadcasted_iota(jnp.int32, (TILE, HD), 0)
                live = row < length
                value = y_ref[at, c, 2].reshape(TILE, HD)
                v_ref[to, :HD] = jnp.where(live, value, jnp.zeros_like(value))
                v_ref[to, HD:] = jnp.where(live, 1.0, 0.0).astype(jnp.bfloat16)

            @pl.when(t >= live_tiles)
            def _(at=at):
                o_ref[at, c] = jnp.zeros((per_tile, rows, HD), jnp.bfloat16)

        for n in range(1, tiles + 1):

            @pl.when(live_tiles == n)
            def _(n=n):
                keys = k_ref[: n * TILE]
                values = v_ref[: n * TILE]
                for t in range(n):
                    scores = lax.dot_general(
                        q_ref[t * TILE : (t + 1) * TILE],
                        keys,
                        (((1,), (1,)), ((), ())),
                        preferred_element_type=jnp.float32,
                    )
                    raised = jnp.exp2(scores * SCALE).astype(jnp.bfloat16)
                    summed = jnp.dot(raised, values, preferred_element_type=jnp.float32)
                    result = summed[:, :HD] / summed[:, HD:]
                    if t == n - 1:
                        row = t * TILE + lax.broadcasted_iota(jnp.int32, (TILE, HD), 0)
                        result = jnp.where(row < length, result, 0.0)
                    o_ref[t * per_tile : (t + 1) * per_tile, c] = result.astype(
                        jnp.bfloat16
                    ).reshape(per_tile, rows, HD)


def attention(meta, y, q_gain, k_gain, first, count):
    blocks, rows = y.shape[0], y.shape[3]
    total = blocks * rows
    vmem = pl.BlockSpec(memory_space=pltpu.VMEM)
    return pl.pallas_call(
        functools.partial(attention_kernel, first, count),
        in_specs=[pl.BlockSpec(memory_space=pltpu.SMEM), vmem, vmem, vmem],
        out_specs=vmem,
        out_shape=pltpu.VMEM((blocks, count, rows, HD), jnp.bfloat16),
        scratch_shapes=[
            pltpu.VMEM((total, HD), jnp.bfloat16),
            pltpu.VMEM((total, HD), jnp.bfloat16),
            pltpu.VMEM((total, 2 * HD), jnp.bfloat16),
        ],
        compiler_params=params(),
        cost_estimate=pl.CostEstimate(
            flops=count * 4 * total * total * HD,
            bytes_accessed=count * total * HD * 8,
            transcendentals=count * total * total,
        ),
        name="attention",
    )(meta, in_vmem(y), q_gain, k_gain)


def project_kernel(first, count, meta_ref, z_ref, w_ref, gate_ref, *refs):
    token_refs, out_refs, a_ref = refs[:count], refs[count : 2 * count], refs[2 * count]
    rows = z_ref.shape[2]

    @pl.when(pl.program_id(0) == 0)
    def _():
        for c in range(count):
            for h in range(HEADS):
                a_ref[c * rows : (c + 1) * rows, h * HD : (h + 1) * HD] = z_ref[h, c]

    projected = jnp.dot(a_ref[...], w_ref[...], preferred_element_type=jnp.float32)
    for c in range(count):
        gate = gate_ref[pl.ds(meta_ref[2 * CG + first + c], 1), :]
        part = projected[c * rows : (c + 1) * rows]
        out_refs[c][...] = (token_refs[c][0].astype(jnp.float32) + gate * part).astype(
            jnp.bfloat16
        )


def project(meta, z, out_weight, gate_table, tokens, first, count):
    rows, width = tokens.shape[1], tokens.shape[2]
    block = 512

    def token_block(c):
        return pl.BlockSpec((1, rows, block), lambda n, m: (m[first + c], 0, n))

    return pl.pallas_call(
        functools.partial(project_kernel, first, count),
        grid_spec=pltpu.PrefetchScalarGridSpec(
            num_scalar_prefetch=1,
            grid=(width // block,),
            in_specs=[
                pl.BlockSpec(memory_space=pltpu.VMEM),
                pl.BlockSpec((HEADS * HD, block), lambda n, m: (0, n)),
                pl.BlockSpec((gate_table.shape[0], block), lambda n, m: (0, n)),
            ]
            + [token_block(c) for c in range(count)],
            out_specs=[pl.BlockSpec((rows, block), lambda n, m: (0, n))] * count,
            scratch_shapes=[pltpu.VMEM((count * rows, HEADS * HD), jnp.bfloat16)],
        ),
        out_shape=[jax.ShapeDtypeStruct((rows, width), jnp.bfloat16)] * count,
        compiler_params=params(),
        cost_estimate=pl.CostEstimate(
            flops=2 * count * rows * HEADS * HD * width,
            bytes_accessed=2 * HEADS * HD * width + 4 * count * rows * width,
            transcendentals=0,
        ),
        name="project",
    )(meta, in_vmem(z), out_weight, gate_table, *[tokens] * count)


def per_device(qkv, tokens, lengths, t_index, slot_target, gate_table, q_gain, k_gain, out_weight):
    groups = lax.axis_size("grp")
    x = jnp.swapaxes(qkv, 1, 2)
    q_gain, k_gain = q_gain.reshape(1, HD), k_gain.reshape(1, HD)
    meta = make_meta(lax.axis_index("grp").reshape(1), lengths, t_index, slot_target)

    last = None

    def exchange(array):
        nonlocal last
        if last is not None:
            array, _ = lax.optimization_barrier((array, last))
        last = lax.all_to_all(array, "sp", split_axis=0, concat_axis=0, tiled=True)
        return last

    out = jnp.zeros_like(tokens)

    def finish(chunk, attended):
        nonlocal out
        z = exchange(attended)
        results = project(meta, z, out_weight, gate_table, tokens, *chunk)
        for c, result in enumerate(results):
            k = chunk[0] + c
            if k:
                result = lax.ppermute(result, "grp", [(g, g ^ k) for g in range(groups)])
            out = lax.dynamic_update_slice(out, result[None], (meta[3 * CG + k], 0, 0))

    waiting = None
    for chunk in CHUNKS:
        y = exchange(prep(meta, x, *chunk))
        if waiting is not None:
            finish(*waiting)
        waiting = (chunk, attention(meta, y, q_gain, k_gain, *chunk))
    finish(*waiting)
    return out


def solution(mesh):
    return jax.shard_map(
        per_device,
        mesh=mesh,
        in_specs=(
            P("grp", "sp", None, None),
            P("grp", "sp", None),
            P(),
            P(),
            P(),
            P(),
            P(),
            P(),
            P(),
        ),
        out_specs=P("grp", "sp", None),
        check_vma=False,
    )
```

```python
import math

import jax
import jax.numpy as jnp
from jax import lax
from jax.experimental import pallas as pl
from jax.experimental.pallas import tpu as pltpu
from jax.sharding import Mesh
from jax.sharding import PartitionSpec as P

HEADS = 16
HD = 128
CG = 8
TILE = 256
SCALE = math.log2(math.e) / math.sqrt(HD)
CORES = 2
SOURCE, LENGTH, ORIGIN, SLOT, STEP = (i * CG for i in range(5))


def params(mib):
    return pltpu.CompilerParams(vmem_limit_bytes=mib * 2**20)


def cost(flops, moved):
    return pl.CostEstimate(flops=flops, bytes_accessed=moved, transcendentals=0)


def in_vmem(array):
    return pltpu.with_memory_space_constraint(array, pltpu.VMEM)


def in_hbm(array):
    return pltpu.with_memory_space_constraint(array, pltpu.HBM)


def meta_kernel(group_ref, length_ref, step_ref, slot_ref, meta_ref):
    group = group_ref[0]
    core = group & (CORES - 1)
    for i in range(CG):
        meta_ref[SOURCE + lax.shift_right_logical(slot_ref[group * CG + i], 3)] = i
        meta_ref[ORIGIN + i] = group ^ i
    for c in range(CORES):
        for i in range(CG):
            clip = ((group & ~(CORES - 1)) + c) * CG + i
            target = lax.shift_right_logical(slot_ref[clip], 3)

            @pl.when((target & (CORES - 1)) == core)
            def _(c=c, clip=clip, target=target):
                at = LENGTH + c * (CG // CORES) + lax.shift_right_logical(target, 1)
                meta_ref[at] = length_ref[clip]

    for clip in range(slot_ref.shape[0]):
        slot = slot_ref[clip]

        @pl.when(lax.shift_right_logical(slot, 3) == group)
        def _(slot=slot, clip=clip):
            k = (clip // CG) ^ group
            meta_ref[SLOT + k] = slot & 7
            meta_ref[STEP + k] = step_ref[clip]


def make_meta(group, lengths, t_index, slot_target):
    smem = pl.BlockSpec(memory_space=pltpu.SMEM)
    return pl.pallas_call(
        meta_kernel,
        out_shape=jax.ShapeDtypeStruct((5 * CG,), jnp.int32),
        in_specs=[smem] * 4,
        out_specs=smem,
        name="meta",
    )(group, lengths, t_index, slot_target)


def prep_kernel(meta_ref, x_ref, o_ref, held_ref, in_sems, out_sems):
    def arriving(d, h):
        source = x_ref.at[meta_ref[SOURCE + d], :, :, pl.ds(h * HD, HD)]
        return pltpu.make_async_copy(source, held_ref.at[d, h], in_sems.at[d, h])

    def leaving(d):
        return pltpu.make_async_copy(
            held_ref.at[d], o_ref.at[:, d % CORES, d // CORES], out_sems.at[d]
        )

    for d in range(CG):
        for h in range(HEADS):
            arriving(d, h).start()
    for d in range(CG):
        for h in range(HEADS):
            arriving(d, h).wait()
        leaving(d).start()
    for d in range(CG):
        leaving(d).wait()


def prep(meta, x):
    clips, _, rows, _ = x.shape
    anywhere = pl.BlockSpec(memory_space=pl.ANY)
    return pl.pallas_call(
        prep_kernel,
        in_specs=[pl.BlockSpec(memory_space=pltpu.SMEM), anywhere],
        out_specs=anywhere,
        out_shape=pltpu.HBM((HEADS, CORES, clips // CORES, 3, rows, HD), jnp.bfloat16),
        scratch_shapes=[
            pltpu.VMEM((clips, HEADS, 3, rows, HD), jnp.bfloat16),
            pltpu.SemaphoreType.DMA((clips, HEADS)),
            pltpu.SemaphoreType.DMA((clips,)),
        ],
        compiler_params=params(12),
        cost_estimate=cost(0, 4 * math.prod(x.shape)),
        name="prep",
    )(meta, in_hbm(x))


def spread_kernel(meta_ref, tokens_ref, *out_refs):
    for k in range(CG):

        @pl.when(pl.program_id(0) == k)
        def _(k=k):
            out_refs[k][...] = tokens_ref[0]


def spread(meta, tokens):
    rows, width = tokens.shape[1:]
    return pl.pallas_call(
        spread_kernel,
        grid_spec=pltpu.PrefetchScalarGridSpec(
            num_scalar_prefetch=1,
            grid=(CG,),
            in_specs=[
                pl.BlockSpec((1, rows, width), lambda k, m: (m[SOURCE + m[ORIGIN + k]], 0, 0))
            ],
            out_specs=[pl.BlockSpec((rows, width), lambda k, m: (0, 0))] * CG,
        ),
        out_shape=[pltpu.HBM((rows, width), tokens.dtype)] * CG,
        compiler_params=params(12),
        cost_estimate=cost(0, 4 * math.prod(tokens.shape)),
        name="spread",
    )(meta, in_hbm(tokens))


def inverse_root(wide):
    square = wide * wide
    high = square.astype(jnp.bfloat16)
    low = (square - high.astype(jnp.float32)).astype(jnp.bfloat16)
    ones = jnp.ones((2 * HD, HD), jnp.bfloat16)
    total = jnp.dot(
        jnp.concatenate([high, low], axis=1), ones, preferred_element_type=jnp.float32
    )
    return lax.rsqrt(total * (1.0 / HD) + 1e-06)


def attend(n, length, y_ref, gain, o_ref, root_ref, k_ref, v_ref):
    blocks, rows = y_ref.shape[0], y_ref.shape[4]
    per_tile = TILE // rows

    def tile(t, part):
        return y_ref[t * per_tile : (t + 1) * per_tile, 0, 0, part].reshape(TILE, HD)

    row = (n - 1) * TILE + lax.broadcasted_iota(jnp.int32, (TILE, HD), 0)
    live = row < length
    for t in range(n):
        to = slice(t * TILE, (t + 1) * TILE)
        root_ref[to] = inverse_root(tile(t, 0).astype(jnp.float32)) * SCALE
        wide = tile(t, 1).astype(jnp.float32)
        k_ref[to] = (wide * inverse_root(wide) * gain).astype(jnp.bfloat16)
        if t < n - 1:
            v_ref[to, :HD] = tile(t, 2)
            v_ref[to, HD:] = jnp.ones((TILE, HD), jnp.bfloat16)
        else:
            factor = jnp.where(live, 1.0, 0.0).astype(jnp.bfloat16)
            v_ref[to, :HD] = tile(t, 2) * factor
            v_ref[to, HD:] = factor
    for t in range(n):
        scores = lax.dot_general(
            tile(t, 0),
            k_ref[: n * TILE],
            (((1,), (1,)), ((), ())),
            preferred_element_type=jnp.float32,
        )
        root = root_ref[t * TILE : (t + 1) * TILE]
        raised = jnp.concatenate(
            [
                jnp.exp2(scores[:, i : i + HD] * root).astype(jnp.bfloat16)
                for i in range(0, n * TILE, HD)
            ],
            axis=1,
        )
        summed = jnp.dot(raised, v_ref[: n * TILE], preferred_element_type=jnp.float32)
        result = summed[:, :HD] / summed[:, HD:]
        if t == n - 1:
            result = jnp.where(live, result, 0.0)
        o_ref[0, t * per_tile : (t + 1) * per_tile, 0] = result.astype(jnp.bfloat16).reshape(
            per_tile, rows, HD
        )
    if n * per_tile < blocks:
        o_ref[0, n * per_tile :, 0] = jnp.zeros((blocks - n * per_tile, rows, HD), jnp.bfloat16)


def attention(meta, y, q_gain, k_gain):
    blocks, cores, count, parts, rows, _ = y.shape
    total = blocks * rows

    def kernel(meta_ref, y_ref, qg_ref, kg_ref, o_ref, *scratch):
        length = meta_ref[LENGTH + pl.program_id(0) * count + pl.program_id(1)]
        live_tiles = lax.div(length + (TILE - 1), TILE)
        gain = qg_ref[...] * kg_ref[...]
        for n in range(1, total // TILE + 1):

            @pl.when(live_tiles == n)
            def _(n=n):
                attend(n, length, y_ref, gain, o_ref, *scratch)

    return pl.pallas_call(
        kernel,
        grid_spec=pltpu.PrefetchScalarGridSpec(
            num_scalar_prefetch=1,
            grid=(cores, count),
            in_specs=[
                pl.BlockSpec((blocks, 1, 1, parts, rows, HD), lambda c, j, m: (0, c, j, 0, 0, 0)),
                pl.BlockSpec((1, HD), lambda c, j, m: (0, 0)),
                pl.BlockSpec((1, HD), lambda c, j, m: (0, 0)),
            ],
            out_specs=pl.BlockSpec((1, blocks, 1, rows, HD), lambda c, j, m: (j, 0, c, 0, 0)),
            scratch_shapes=[
                pltpu.VMEM((total, HD), jnp.float32),
                pltpu.VMEM((total, HD), jnp.bfloat16),
                pltpu.VMEM((total, 2 * HD), jnp.bfloat16),
            ],
        ),
        out_shape=pltpu.HBM((count, blocks, cores, rows, HD), jnp.bfloat16),
        compiler_params=params(24),
        cost_estimate=cost(
            cores * count * 4 * total * total * HD, cores * count * total * HD * 8
        ),
        name="attention",
    )(meta, in_hbm(y), q_gain, k_gain)


def project(meta, z, out_weight, gate_table, tokens):
    rows, width = tokens[0].shape
    clips, block = len(tokens), 512
    steps = width // block

    def kernel(meta_ref, z_ref, weight_ref, gate_ref, *refs):
        token_refs, (out_ref, a_ref, w_ref, sems) = refs[:clips], refs[clips:]

        def arriving(n):
            columns = pl.ds(n * block, block)
            return pltpu.make_async_copy(weight_ref.at[:, columns], w_ref.at[n], sems.at[n])

        @pl.when(pl.program_id(0) == 0)
        def _():
            for n in range(steps):
                arriving(n).start()
            for k in range(clips):
                origin = meta_ref[ORIGIN + k]
                x, core = lax.shift_right_logical(origin, 1), origin & (CORES - 1)
                for h in range(HEADS):
                    a_ref[k * rows : (k + 1) * rows, h * HD : (h + 1) * HD] = z_ref[x, h, core]

        for n in range(steps):

            @pl.when(pl.program_id(0) == n)
            def _(n=n):
                arriving(n).wait()

        projected = jnp.dot(
            a_ref[...], w_ref[pl.program_id(0)], preferred_element_type=jnp.float32
        )
        for k in range(clips):
            gate = gate_ref[pl.ds(meta_ref[STEP + k], 1), :]
            part = gate * projected[k * rows : (k + 1) * rows]
            out_ref[meta_ref[SLOT + k]] = (token_refs[k][...].astype(jnp.float32) + part).astype(
                jnp.bfloat16
            )

    return pl.pallas_call(
        kernel,
        grid_spec=pltpu.PrefetchScalarGridSpec(
            num_scalar_prefetch=1,
            grid=(steps,),
            in_specs=[
                pl.BlockSpec(memory_space=pltpu.VMEM),
                pl.BlockSpec(memory_space=pl.ANY),
                pl.BlockSpec((gate_table.shape[0], block), lambda n, m: (0, n)),
            ]
            + [pl.BlockSpec((rows, block), lambda n, m: (0, n))] * clips,
            out_specs=pl.BlockSpec((clips, rows, block), lambda n, m: (0, 0, n)),
            scratch_shapes=[
                pltpu.VMEM((clips * rows, HEADS * HD), jnp.bfloat16),
                pltpu.VMEM((steps, HEADS * HD, block), jnp.bfloat16),
                pltpu.SemaphoreType.DMA((steps,)),
            ],
        ),
        out_shape=pltpu.HBM((clips, rows, width), jnp.bfloat16),
        compiler_params=params(40),
        cost_estimate=cost(
            2 * clips * rows * HEADS * HD * width,
            2 * HEADS * HD * width + 4 * clips * rows * width,
        ),
        name="project",
    )(
        meta,
        in_vmem(z),
        in_hbm(out_weight),
        in_hbm(gate_table),
        *[in_hbm(part) for part in tokens],
    )


def per_device(qkv, tokens, lengths, t_index, slot_target, gate_table, q_gain, k_gain, out_weight):
    group = lax.axis_index(("x", "core"))
    meta = make_meta(group.reshape(1), lengths, t_index, slot_target)

    def across(part, k):
        pairs = [(g, g ^ k) for g in range(CG)]
        return lax.ppermute(part, ("x", "core"), pairs) if k else part

    def exchange(array, axes, kept):
        sent = array.reshape(-1, *array.shape[kept:])
        arrived = lax.all_to_all(sent, axes, split_axis=0, concat_axis=0, tiled=True)
        return arrived.reshape(array.shape)

    y = exchange(prep(meta, jnp.swapaxes(qkv, 1, 2)), ("z", "y", "core"), 2)
    resid = [across(part, k) for k, part in enumerate(spread(meta, tokens))]
    y, *resid = lax.optimization_barrier((y, *resid))
    attended = attention(meta, y, q_gain.reshape(1, HD), k_gain.reshape(1, HD))
    z = exchange(attended, ("x", "z", "y"), 2)
    return project(meta, z, out_weight, gate_table, resid)


def solution(mesh):
    apart = Mesh(mesh.devices.reshape(CG // CORES, CORES, 4, 4), ("x", "core", "z", "y"))
    clips, tokens = ("x", "core"), ("z", "y")
    return jax.shard_map(
        per_device,
        mesh=apart,
        in_specs=(
            P(clips, tokens, None, None),
            P(clips, tokens, None),
            P(),
            P(),
            P(),
            P(),
            P(),
            P(),
            P(),
        ),
        out_specs=P(clips, tokens, None),
        check_vma=False,
    )
```

```python
import math

import jax
import jax.numpy as jnp
from jax import lax
from jax.experimental import pallas as pl
from jax.experimental.pallas import tpu as pltpu
from jax.sharding import Mesh
from jax.sharding import PartitionSpec as P

HEADS = 16
HD = 128
CG = 8
TILE = 256
SCALE = math.log2(math.e) / math.sqrt(HD)
CORES = 2
GROUPS = CG // CORES
SOURCE, LENGTH, ORIGIN, SLOT, STEP = (i * CG for i in range(5))


def params(mib):
    return pltpu.CompilerParams(vmem_limit_bytes=mib * 2**20)


def cost(flops, moved):
    return pl.CostEstimate(flops=flops, bytes_accessed=moved, transcendentals=0)


def in_vmem(array):
    return pltpu.with_memory_space_constraint(array, pltpu.VMEM)


def in_hbm(array):
    return pltpu.with_memory_space_constraint(array, pltpu.HBM)


def meta_kernel(group_ref, length_ref, step_ref, slot_ref, meta_ref):
    group = group_ref[0]
    core = group & (CORES - 1)
    for i in range(CG):
        meta_ref[SOURCE + lax.shift_right_logical(slot_ref[group * CG + i], 3)] = i
        meta_ref[ORIGIN + i] = group ^ i
    for c in range(CORES):
        for i in range(CG):
            clip = ((group & ~(CORES - 1)) + c) * CG + i
            target = lax.shift_right_logical(slot_ref[clip], 3)

            @pl.when((target & (CORES - 1)) == core)
            def _(c=c, clip=clip, target=target):
                at = LENGTH + c * (CG // CORES) + lax.shift_right_logical(target, 1)
                meta_ref[at] = length_ref[clip]

    for clip in range(slot_ref.shape[0]):
        slot = slot_ref[clip]

        @pl.when(lax.shift_right_logical(slot, 3) == group)
        def _(slot=slot, clip=clip):
            k = (clip // CG) ^ group
            meta_ref[SLOT + k] = slot & 7
            meta_ref[STEP + k] = step_ref[clip]


def make_meta(group, lengths, t_index, slot_target):
    smem = pl.BlockSpec(memory_space=pltpu.SMEM)
    return pl.pallas_call(
        meta_kernel,
        out_shape=jax.ShapeDtypeStruct((5 * CG,), jnp.int32),
        in_specs=[smem] * 4,
        out_specs=smem,
        name="meta",
    )(group, lengths, t_index, slot_target)


def prep(group, slot_target, x):
    clips, _, rows, _ = x.shape
    targets = range(clips)
    ahead = 3

    def kernel(group_ref, slot_ref, x_ref, o_ref, held_ref, in_sems, out_sems):
        base = group_ref[0] * clips
        own = [lax.shift_right_logical(slot_ref[base + i], 3) for i in range(clips)]

        def source(target):
            return sum(jnp.where(own[i] == target, i, 0) for i in range(1, clips))

        sources = [source(target) for target in targets]

        def arriving(n, h):
            columns = x_ref.at[sources[n], :, :, pl.ds(h * HD, HD)]
            return pltpu.make_async_copy(columns, held_ref.at[n, h], in_sems.at[n])

        def all_of(n):
            return pltpu.make_async_copy(held_ref.at[n], held_ref.at[n], in_sems.at[n])

        def leaving(n):
            to = o_ref.at[:, n % CORES, n // CORES]
            return pltpu.make_async_copy(held_ref.at[n], to, out_sems.at[n])

        for n in range(len(targets) + ahead):
            if n < len(targets):
                for h in range(HEADS):
                    arriving(n, h).start()
            if n >= ahead:
                all_of(n - ahead).wait()
                leaving(n - ahead).start()
        for n in range(len(targets)):
            leaving(n).wait()

    smem = pl.BlockSpec(memory_space=pltpu.SMEM)
    anywhere = pl.BlockSpec(memory_space=pl.ANY)
    return pl.pallas_call(
        kernel,
        in_specs=[smem, smem, anywhere],
        out_specs=anywhere,
        out_shape=pltpu.HBM((HEADS, CORES, GROUPS, 3, rows, HD), jnp.bfloat16),
        scratch_shapes=[
            pltpu.VMEM((len(targets), HEADS, 3, rows, HD), jnp.bfloat16),
            pltpu.SemaphoreType.DMA((len(targets),)),
            pltpu.SemaphoreType.DMA((len(targets),)),
        ],
        compiler_params=params(12),
        cost_estimate=cost(0, len(targets) * 12 * rows * HEADS * HD),
        name="prep",
    )(group, slot_target, in_hbm(x))


def spread_kernel(meta_ref, tokens_ref, *out_refs):
    for k in range(CG):

        @pl.when(pl.program_id(0) == k)
        def _(k=k):
            out_refs[k][...] = tokens_ref[0]


def spread(meta, tokens):
    rows, width = tokens.shape[1:]
    return pl.pallas_call(
        spread_kernel,
        grid_spec=pltpu.PrefetchScalarGridSpec(
            num_scalar_prefetch=1,
            grid=(CG,),
            in_specs=[
                pl.BlockSpec((1, rows, width), lambda k, m: (m[SOURCE + m[ORIGIN + k]], 0, 0))
            ],
            out_specs=[pl.BlockSpec((rows, width), lambda k, m: (0, 0))] * CG,
        ),
        out_shape=[pltpu.HBM((rows, width), tokens.dtype)] * CG,
        compiler_params=params(12),
        cost_estimate=cost(0, 4 * math.prod(tokens.shape)),
        name="spread",
    )(meta, in_hbm(tokens))


def inverse_root(wide):
    return lax.rsqrt(jnp.mean(wide * wide, axis=-1, keepdims=True) + 1e-06)


def attend(n, length, tile, store, gain, root_ref, k_ref, v_ref):
    row = (n - 1) * TILE + lax.broadcasted_iota(jnp.int32, (TILE, HD), 0)
    live = row < length
    for t in range(n):
        to = slice(t * TILE, (t + 1) * TILE)
        root = inverse_root(tile(t, 0).astype(jnp.float32)) * SCALE
        root_ref[to] = jnp.broadcast_to(root, (TILE, HD))
        wide = tile(t, 1).astype(jnp.float32)
        k_ref[to] = (wide * inverse_root(wide) * gain).astype(jnp.bfloat16)
        if t < n - 1:
            v_ref[to, :HD] = tile(t, 2)
            v_ref[to, HD:] = jnp.ones((TILE, HD), jnp.bfloat16)
        else:
            factor = jnp.where(live, 1.0, 0.0).astype(jnp.bfloat16)
            v_ref[to, :HD] = tile(t, 2) * factor
            v_ref[to, HD:] = factor
    for t in range(n):
        scores = lax.dot_general(
            tile(t, 0),
            k_ref[: n * TILE],
            (((1,), (1,)), ((), ())),
            preferred_element_type=jnp.float32,
        )
        root = root_ref[t * TILE : (t + 1) * TILE]
        raised = jnp.concatenate(
            [
                jnp.exp2(scores[:, i : i + HD] * root).astype(jnp.bfloat16)
                for i in range(0, n * TILE, HD)
            ],
            axis=1,
        )
        summed = jnp.dot(raised, v_ref[: n * TILE], preferred_element_type=jnp.float32)
        result = summed[:, :HD] / summed[:, HD:]
        if t == n - 1:
            result = jnp.where(live, result, 0.0)
        store(t, result.astype(jnp.bfloat16))


def attention(meta, y, q_gain, k_gain):
    blocks, cores, groups, parts, rows, _ = y.shape
    total = blocks * rows
    per_tile, tiles = TILE // rows, total // TILE

    clips = cores * groups

    def kernel(meta_ref, y_ref, qg_ref, kg_ref, o_ref, held_ref, sems, *scratch):
        gain = qg_ref[...] * kg_ref[...]

        def arriving(i):
            clip = y_ref.at[:, lax.div(i, groups), lax.rem(i, groups)]
            return pltpu.make_async_copy(clip, held_ref.at[i], sems.at[i])

        for i in range(clips):
            arriving(i).start()

        def one_clip(i, carry):
            arriving(i).wait()
            c, x = lax.div(i, groups), lax.rem(i, groups)
            length = meta_ref[LENGTH + i]
            live_tiles = lax.div(length + (TILE - 1), TILE)

            def tile(t, part):
                at = slice(t * per_tile, (t + 1) * per_tile)
                return held_ref[i, at, part].reshape(TILE, HD)

            def store(t, result):
                at = slice(t * per_tile, (t + 1) * per_tile)
                o_ref[x, at, c] = result.reshape(per_tile, rows, HD)

            for n in range(1, tiles + 1):

                @pl.when(live_tiles == n)
                def _(n=n):
                    attend(n, length, tile, store, gain, *scratch)
                    for t in range(n, tiles):
                        store(t, jnp.zeros((TILE, HD), jnp.bfloat16))

            return carry

        lax.fori_loop(0, clips, one_clip, 0)

    vmem = pl.BlockSpec(memory_space=pltpu.VMEM)
    return pl.pallas_call(
        kernel,
        in_specs=[
            pl.BlockSpec(memory_space=pltpu.SMEM),
            pl.BlockSpec(memory_space=pl.ANY),
            vmem,
            vmem,
        ],
        out_specs=vmem,
        out_shape=pltpu.VMEM((groups, blocks, cores, rows, HD), jnp.bfloat16),
        scratch_shapes=[
            pltpu.VMEM((clips, blocks, parts, rows, HD), jnp.bfloat16),
            pltpu.SemaphoreType.DMA((clips,)),
            pltpu.VMEM((total, HD), jnp.float32),
            pltpu.VMEM((total, HD), jnp.bfloat16),
            pltpu.VMEM((total, 2 * HD), jnp.bfloat16),
        ],
        compiler_params=params(24),
        cost_estimate=cost(clips * 4 * total * total * HD, clips * total * HD * 8),
        name="attention",
    )(meta, in_hbm(y), q_gain, k_gain)


def load(weight):
    def kernel(from_ref, to_ref, sem):
        copy = pltpu.make_async_copy(from_ref, to_ref, sem)
        copy.start()
        copy.wait()

    return pl.pallas_call(
        kernel,
        in_specs=[pl.BlockSpec(memory_space=pl.ANY)],
        out_specs=pl.BlockSpec(memory_space=pltpu.VMEM),
        out_shape=pltpu.VMEM(weight.shape, weight.dtype),
        scratch_shapes=[pltpu.SemaphoreType.DMA],
        compiler_params=params(16),
        cost_estimate=cost(0, 4 * math.prod(weight.shape)),
        name="load",
    )(in_hbm(weight))


def project(meta, z, out_weight, gate_table, tokens):
    rows, width = tokens[0].shape
    clips, block = len(tokens), 512
    steps = width // block

    def kernel(meta_ref, z_ref, w_ref, gate_ref, *refs):
        token_refs, (out_ref, a_ref) = refs[:clips], refs[clips:]

        @pl.when(pl.program_id(0) == 0)
        def _():
            for k in range(clips):
                origin = meta_ref[ORIGIN + k]
                x, core = lax.shift_right_logical(origin, 1), origin & (CORES - 1)
                for h in range(HEADS):
                    a_ref[k * rows : (k + 1) * rows, h * HD : (h + 1) * HD] = z_ref[x, h, core]

        columns = pl.ds(pl.multiple_of(pl.program_id(0) * block, block), block)
        projected = jnp.dot(a_ref[...], w_ref[:, columns], preferred_element_type=jnp.float32)
        for k in range(clips):
            gate = gate_ref[pl.ds(meta_ref[STEP + k], 1), :]
            part = gate * projected[k * rows : (k + 1) * rows]
            out_ref[meta_ref[SLOT + k]] = (token_refs[k][...].astype(jnp.float32) + part).astype(
                jnp.bfloat16
            )

    return pl.pallas_call(
        kernel,
        grid_spec=pltpu.PrefetchScalarGridSpec(
            num_scalar_prefetch=1,
            grid=(steps,),
            in_specs=[
                pl.BlockSpec(memory_space=pltpu.VMEM),
                pl.BlockSpec(memory_space=pltpu.VMEM),
                pl.BlockSpec((gate_table.shape[0], block), lambda n, m: (0, n)),
            ]
            + [pl.BlockSpec((rows, block), lambda n, m: (0, n))] * clips,
            out_specs=pl.BlockSpec((clips, rows, block), lambda n, m: (0, 0, n)),
            scratch_shapes=[pltpu.VMEM((clips * rows, HEADS * HD), jnp.bfloat16)],
        ),
        out_shape=pltpu.HBM((clips, rows, width), jnp.bfloat16),
        compiler_params=params(24),
        cost_estimate=cost(
            2 * clips * rows * HEADS * HD * width,
            2 * HEADS * HD * width + 4 * clips * rows * width,
        ),
        name="project",
    )(
        meta,
        in_vmem(z),
        in_vmem(out_weight),
        in_hbm(gate_table),
        *[in_hbm(part) for part in tokens],
    )


def per_device(qkv, tokens, lengths, t_index, slot_target, gate_table, q_gain, k_gain, out_weight):
    group = lax.axis_index(("x", "core"))
    group = group.reshape(1)
    meta = make_meta(group, lengths, t_index, slot_target)

    def across(part, k):
        pairs = [(g, g ^ k) for g in range(CG)]
        return lax.ppermute(part, ("x", "core"), pairs) if k else part

    def exchange(array, axes, kept):
        sent = array.reshape(-1, *array.shape[kept:])
        arrived = lax.all_to_all(sent, axes, split_axis=0, concat_axis=0, tiled=True)
        return arrived.reshape(array.shape)

    resid = [across(part, k) for k, part in enumerate(spread(meta, tokens))]
    weight = load(out_weight)
    y = exchange(prep(group, slot_target, jnp.swapaxes(qkv, 1, 2)), ("z", "y", "core"), 2)
    y, weight, *resid = lax.optimization_barrier((y, weight, *resid))
    attended = attention(meta, y, q_gain.reshape(1, HD), k_gain.reshape(1, HD))
    z = exchange(attended, ("x", "z", "y"), 2)
    return project(meta, z, weight, gate_table, resid)


def solution(mesh):
    apart = Mesh(mesh.devices.reshape(GROUPS, CORES, 4, 4), ("x", "core", "z", "y"))
    clips, tokens = ("x", "core"), ("z", "y")
    return jax.shard_map(
        per_device,
        mesh=apart,
        in_specs=(
            P(clips, tokens, None, None),
            P(clips, tokens, None),
            P(),
            P(),
            P(),
            P(),
            P(),
            P(),
            P(),
        ),
        out_specs=P(clips, tokens, None),
        check_vma=False,
    )
```

```python
import math

import jax
import jax.numpy as jnp
from jax import lax
from jax.experimental import pallas as pl
from jax.experimental.pallas import tpu as pltpu
from jax.sharding import Mesh
from jax.sharding import PartitionSpec as P

HEADS = 16
HD = 128
CG = 8
TILE = 256
SCALE = math.log2(math.e) / math.sqrt(HD)
CORES = 2
GROUPS = CG // CORES
SOURCE, LENGTH, ORIGIN, SLOT, STEP = (i * CG for i in range(5))


def params(mib):
    return pltpu.CompilerParams(vmem_limit_bytes=mib * 2**20)


def cost(flops, moved):
    return pl.CostEstimate(flops=flops, bytes_accessed=moved, transcendentals=0)


def in_vmem(array):
    return pltpu.with_memory_space_constraint(array, pltpu.VMEM)


def in_hbm(array):
    return pltpu.with_memory_space_constraint(array, pltpu.HBM)


def meta_kernel(group_ref, length_ref, step_ref, slot_ref, meta_ref):
    group = group_ref[0]
    core = group & (CORES - 1)
    for i in range(CG):
        meta_ref[SOURCE + lax.shift_right_logical(slot_ref[group * CG + i], 3)] = i
        meta_ref[ORIGIN + i] = group ^ i
    for c in range(CORES):
        for i in range(CG):
            clip = ((group & ~(CORES - 1)) + c) * CG + i
            target = lax.shift_right_logical(slot_ref[clip], 3)

            @pl.when((target & (CORES - 1)) == core)
            def _(c=c, clip=clip, target=target):
                at = LENGTH + c * (CG // CORES) + lax.shift_right_logical(target, 1)
                meta_ref[at] = length_ref[clip]

    for clip in range(slot_ref.shape[0]):
        slot = slot_ref[clip]

        @pl.when(lax.shift_right_logical(slot, 3) == group)
        def _(slot=slot, clip=clip):
            k = (clip // CG) ^ group
            meta_ref[SLOT + k] = slot & 7
            meta_ref[STEP + k] = step_ref[clip]


def make_meta(group, lengths, t_index, slot_target):
    smem = pl.BlockSpec(memory_space=pltpu.SMEM)
    return pl.pallas_call(
        meta_kernel,
        out_shape=jax.ShapeDtypeStruct((5 * CG,), jnp.int32),
        in_specs=[smem] * 4,
        out_specs=smem,
        name="meta",
    )(group, lengths, t_index, slot_target)


def prep(group, slot_target, x):
    clips, _, rows, _ = x.shape
    targets = range(clips)
    ahead = 3

    def kernel(group_ref, slot_ref, x_ref, o_ref, held_ref, in_sems, out_sems):
        base = group_ref[0] * clips
        own = [lax.shift_right_logical(slot_ref[base + i], 3) for i in range(clips)]

        def source(target):
            return sum(jnp.where(own[i] == target, i, 0) for i in range(1, clips))

        sources = [source(target) for target in targets]

        def arriving(n, h):
            columns = x_ref.at[sources[n], :, :, pl.ds(h * HD, HD)]
            return pltpu.make_async_copy(columns, held_ref.at[n, h], in_sems.at[n])

        def all_of(n):
            return pltpu.make_async_copy(held_ref.at[n], held_ref.at[n], in_sems.at[n])

        def leaving(n):
            to = o_ref.at[:, n % CORES, n // CORES]
            return pltpu.make_async_copy(held_ref.at[n], to, out_sems.at[n])

        for n in range(len(targets) + ahead):
            if n < len(targets):
                for h in range(HEADS):
                    arriving(n, h).start()
            if n >= ahead:
                all_of(n - ahead).wait()
                leaving(n - ahead).start()
        for n in range(len(targets)):
            leaving(n).wait()

    smem = pl.BlockSpec(memory_space=pltpu.SMEM)
    anywhere = pl.BlockSpec(memory_space=pl.ANY)
    return pl.pallas_call(
        kernel,
        in_specs=[smem, smem, anywhere],
        out_specs=anywhere,
        out_shape=pltpu.HBM((HEADS, CORES, GROUPS, 3, rows, HD), jnp.bfloat16),
        scratch_shapes=[
            pltpu.VMEM((len(targets), HEADS, 3, rows, HD), jnp.bfloat16),
            pltpu.SemaphoreType.DMA((len(targets),)),
            pltpu.SemaphoreType.DMA((len(targets),)),
        ],
        compiler_params=params(12),
        cost_estimate=cost(0, len(targets) * 12 * rows * HEADS * HD),
        name="prep",
    )(in_hbm(group), in_hbm(slot_target), in_hbm(x))


def spread_kernel(meta_ref, tokens_ref, *out_refs):
    for k in range(CG):

        @pl.when(pl.program_id(0) == k)
        def _(k=k):
            out_refs[k][...] = tokens_ref[0]


def spread(meta, tokens):
    rows, width = tokens.shape[1:]
    return pl.pallas_call(
        spread_kernel,
        grid_spec=pltpu.PrefetchScalarGridSpec(
            num_scalar_prefetch=1,
            grid=(CG,),
            in_specs=[
                pl.BlockSpec((1, rows, width), lambda k, m: (m[SOURCE + m[ORIGIN + k]], 0, 0))
            ],
            out_specs=[pl.BlockSpec((rows, width), lambda k, m: (0, 0))] * CG,
        ),
        out_shape=[pltpu.HBM((rows, width), tokens.dtype)] * CG,
        compiler_params=params(12),
        cost_estimate=cost(0, 4 * math.prod(tokens.shape)),
        name="spread",
    )(meta, in_hbm(tokens))


def inverse_root(wide):
    return lax.rsqrt(jnp.mean(wide * wide, axis=-1, keepdims=True) + 1e-06)


def attend(n, length, tile, store, gain, root_ref, k_ref, v_ref):
    row = (n - 1) * TILE + lax.broadcasted_iota(jnp.int32, (TILE, HD), 0)
    live = row < length
    for t in range(n):
        to = slice(t * TILE, (t + 1) * TILE)
        root = inverse_root(tile(t, 0).astype(jnp.float32)) * SCALE
        root_ref[to] = jnp.broadcast_to(root, (TILE, HD))
        wide = tile(t, 1).astype(jnp.float32)
        k_ref[to] = (wide * inverse_root(wide) * gain).astype(jnp.bfloat16)
        if t < n - 1:
            v_ref[to, :HD] = tile(t, 2)
            v_ref[to, HD:] = jnp.ones((TILE, HD), jnp.bfloat16)
        else:
            factor = jnp.where(live, 1.0, 0.0).astype(jnp.bfloat16)
            v_ref[to, :HD] = tile(t, 2) * factor
            v_ref[to, HD:] = factor

    def scores_of(t):
        return lax.dot_general(
            tile(t, 0),
            k_ref[: n * TILE],
            (((1,), (1,)), ((), ())),
            preferred_element_type=jnp.float32,
        )

    ahead = [scores_of(t) for t in range(min(2, n))]
    for t in range(n):
        scores = ahead.pop(0)
        if t + 2 < n:
            ahead.append(scores_of(t + 2))
        root = root_ref[t * TILE : (t + 1) * TILE]
        raised = jnp.concatenate(
            [
                jnp.exp2(scores[:, i : i + HD] * root).astype(jnp.bfloat16)
                for i in range(0, n * TILE, HD)
            ],
            axis=1,
        )
        summed = jnp.dot(raised, v_ref[: n * TILE], preferred_element_type=jnp.float32)
        result = summed[:, :HD] / summed[:, HD:]
        if t == n - 1:
            result = jnp.where(live, result, 0.0)
        store(t, result.astype(jnp.bfloat16))


def attention(meta, y, q_gain, k_gain):
    blocks, cores, groups, parts, rows, _ = y.shape
    total = blocks * rows
    per_tile, tiles = TILE // rows, total // TILE

    clips = cores * groups

    def kernel(meta_ref, y_ref, qg_ref, kg_ref, o_ref, held_ref, sems, *scratch):
        gain = qg_ref[...] * kg_ref[...]

        def arriving(i):
            clip = y_ref.at[:, lax.div(i, groups), lax.rem(i, groups)]
            return pltpu.make_async_copy(clip, held_ref.at[i], sems.at[i])

        for i in range(clips):
            arriving(i).start()

        def one_clip(i, carry):
            arriving(i).wait()
            c, x = lax.div(i, groups), lax.rem(i, groups)
            length = meta_ref[LENGTH + i]
            live_tiles = lax.div(length + (TILE - 1), TILE)

            def tile(t, part):
                at = slice(t * per_tile, (t + 1) * per_tile)
                return held_ref[i, at, part].reshape(TILE, HD)

            def store(t, result):
                at = slice(t * per_tile, (t + 1) * per_tile)
                o_ref[at, x, c] = result.reshape(per_tile, rows, HD)

            for n in range(1, tiles + 1):

                @pl.when(live_tiles == n)
                def _(n=n):
                    attend(n, length, tile, store, gain, *scratch)
                    for t in range(n, tiles):
                        store(t, jnp.zeros((TILE, HD), jnp.bfloat16))

            return carry

        lax.fori_loop(0, clips, one_clip, 0)

    vmem = pl.BlockSpec(memory_space=pltpu.VMEM)
    return pl.pallas_call(
        kernel,
        in_specs=[
            pl.BlockSpec(memory_space=pltpu.SMEM),
            pl.BlockSpec(memory_space=pl.ANY),
            vmem,
            vmem,
        ],
        out_specs=vmem,
        out_shape=pltpu.VMEM((blocks, groups, cores, rows, HD), jnp.bfloat16),
        scratch_shapes=[
            pltpu.VMEM((clips, blocks, parts, rows, HD), jnp.bfloat16),
            pltpu.SemaphoreType.DMA((clips,)),
            pltpu.VMEM((total, HD), jnp.float32),
            pltpu.VMEM((total, HD), jnp.bfloat16),
            pltpu.VMEM((total, 2 * HD), jnp.bfloat16),
        ],
        compiler_params=params(24),
        cost_estimate=cost(clips * 4 * total * total * HD, clips * total * HD * 8),
        name="attention",
    )(meta, in_hbm(y), q_gain, k_gain)


def load(weight):
    def kernel(from_ref, to_ref, sem):
        copy = pltpu.make_async_copy(from_ref, to_ref, sem)
        copy.start()
        copy.wait()

    return pl.pallas_call(
        kernel,
        in_specs=[pl.BlockSpec(memory_space=pl.ANY)],
        out_specs=pl.BlockSpec(memory_space=pltpu.VMEM),
        out_shape=pltpu.VMEM(weight.shape, weight.dtype),
        scratch_shapes=[pltpu.SemaphoreType.DMA],
        compiler_params=params(16),
        cost_estimate=cost(0, 4 * math.prod(weight.shape)),
        name="load",
    )(in_hbm(weight))


def project(meta, z, weight, gate_table, tokens):
    rows, width = tokens[0].shape
    clips, block = len(tokens), 512
    steps = width // block

    def kernel(meta_ref, z_ref, w_ref, gate_ref, *refs):
        token_refs = refs[:clips]
        out_ref, a_ref, rate_ref, resid_ref, held_ref, in_sems, out_sems = refs[clips:]
        arriving = [
            pltpu.make_async_copy(token_refs[k], resid_ref.at[k], in_sems.at[k])
            for k in range(clips)
        ] + [pltpu.make_async_copy(gate_ref, rate_ref, in_sems.at[clips])]
        for copy in arriving:
            copy.start()
        for k in range(clips):
            origin = meta_ref[ORIGIN + k]
            x, core = lax.shift_right_logical(origin, 1), origin & (CORES - 1)
            for h in range(HEADS):
                a_ref[k * rows : (k + 1) * rows, h * HD : (h + 1) * HD] = z_ref[h, x, core]
        for copy in arriving:
            copy.wait()

        def leaving(n, columns):
            return pltpu.make_async_copy(
                held_ref.at[n], out_ref.at[:, :, columns], out_sems.at[n]
            )

        for n in range(steps):
            columns = pl.ds(n * block, block)
            projected = jnp.dot(a_ref[...], w_ref[:, columns], preferred_element_type=jnp.float32)
            for k in range(clips):
                gate = rate_ref[pl.ds(meta_ref[STEP + k], 1), columns]
                part = gate * projected[k * rows : (k + 1) * rows]
                total = resid_ref[k, :, columns].astype(jnp.float32) + part
                held_ref[n, meta_ref[SLOT + k]] = total.astype(jnp.bfloat16)
            leaving(n, columns).start()
        for n in range(steps):
            leaving(n, pl.ds(n * block, block)).wait()

    smem, vmem, anywhere = (
        pl.BlockSpec(memory_space=space) for space in (pltpu.SMEM, pltpu.VMEM, pl.ANY)
    )
    return pl.pallas_call(
        kernel,
        in_specs=[smem, vmem, vmem, anywhere] + [anywhere] * clips,
        out_specs=anywhere,
        out_shape=pltpu.HBM((clips, rows, width), jnp.bfloat16),
        scratch_shapes=[
            pltpu.VMEM((clips * rows, HEADS * HD), jnp.bfloat16),
            pltpu.VMEM(gate_table.shape, jnp.float32),
            pltpu.VMEM((clips, rows, width), jnp.bfloat16),
            pltpu.VMEM((steps, clips, rows, block), jnp.bfloat16),
            pltpu.SemaphoreType.DMA((clips + 1,)),
            pltpu.SemaphoreType.DMA((steps,)),
        ],
        compiler_params=params(24),
        cost_estimate=cost(
            2 * clips * rows * HEADS * HD * width,
            2 * HEADS * HD * width + 4 * clips * rows * width,
        ),
        name="project",
    )(
        meta,
        in_vmem(z),
        in_vmem(weight),
        in_hbm(gate_table),
        *[in_hbm(part) for part in tokens],
    )


def per_device(qkv, tokens, lengths, t_index, slot_target, gate_table, q_gain, k_gain, out_weight):
    group = lax.axis_index(("x", "core"))
    group = group.reshape(1)
    meta = make_meta(group, lengths, t_index, slot_target)

    def across(part, k):
        pairs = [(g, g ^ k) for g in range(CG)]
        return lax.ppermute(part, ("x", "core"), pairs) if k else part

    def exchange(array, axes, kept):
        sent = array.reshape(-1, *array.shape[kept:])
        arrived = lax.all_to_all(sent, axes, split_axis=0, concat_axis=0, tiled=True)
        return arrived.reshape(array.shape)

    resid = [across(part, k) for k, part in enumerate(spread(meta, tokens))]
    weight = load(out_weight)
    y = exchange(prep(group, slot_target, jnp.swapaxes(qkv, 1, 2)), ("z", "y", "core"), 2)
    y, weight, *resid = lax.optimization_barrier((y, weight, *resid))
    attended = attention(meta, y, q_gain.reshape(1, HD), k_gain.reshape(1, HD))
    z = exchange(attended, ("z", "y", "x"), 2)
    return project(meta, z, weight, gate_table, resid)


def solution(mesh):
    apart = Mesh(mesh.devices.reshape(GROUPS, CORES, 4, 4), ("x", "core", "z", "y"))
    clips, tokens = ("x", "core"), ("z", "y")
    return jax.shard_map(
        per_device,
        mesh=apart,
        in_specs=(
            P(clips, tokens, None, None),
            P(clips, tokens, None),
            P(),
            P(),
            P(),
            P(),
            P(),
            P(),
            P(),
        ),
        out_specs=P(clips, tokens, None),
        check_vma=False,
    )
```

```python
import math

import jax
import jax.numpy as jnp
from jax import lax
from jax.experimental import pallas as pl
from jax.experimental.pallas import tpu as pltpu
from jax.sharding import Mesh
from jax.sharding import PartitionSpec as P

HEADS = 16
HD = 128
CG = 8
TILE = 256
SCALE = math.log2(math.e) / math.sqrt(HD)
CORES = 2
GROUPS = CG // CORES
SOURCE, LENGTH, ORIGIN, SLOT, STEP = (i * CG for i in range(5))


def params(mib):
    return pltpu.CompilerParams(vmem_limit_bytes=mib * 2**20)


def cost(flops, moved):
    return pl.CostEstimate(flops=flops, bytes_accessed=moved, transcendentals=0)


def in_vmem(array):
    return pltpu.with_memory_space_constraint(array, pltpu.VMEM)


def in_hbm(array):
    return pltpu.with_memory_space_constraint(array, pltpu.HBM)


def meta_kernel(group_ref, length_ref, step_ref, slot_ref, meta_ref):
    group = group_ref[0]
    core = group & (CORES - 1)
    for i in range(CG):
        meta_ref[SOURCE + lax.shift_right_logical(slot_ref[group * CG + i], 3)] = i
        meta_ref[ORIGIN + i] = group ^ i
    for c in range(CORES):
        for i in range(CG):
            clip = ((group & ~(CORES - 1)) + c) * CG + i
            target = lax.shift_right_logical(slot_ref[clip], 3)

            @pl.when((target & (CORES - 1)) == core)
            def _(c=c, clip=clip, target=target):
                at = LENGTH + c * (CG // CORES) + lax.shift_right_logical(target, 1)
                meta_ref[at] = length_ref[clip]

    for clip in range(slot_ref.shape[0]):
        slot = slot_ref[clip]

        @pl.when(lax.shift_right_logical(slot, 3) == group)
        def _(slot=slot, clip=clip):
            k = (clip // CG) ^ group
            meta_ref[SLOT + k] = slot & 7
            meta_ref[STEP + k] = step_ref[clip]


def make_meta(group, lengths, t_index, slot_target):
    smem = pl.BlockSpec(memory_space=pltpu.SMEM)
    return pl.pallas_call(
        meta_kernel,
        out_shape=jax.ShapeDtypeStruct((5 * CG,), jnp.int32),
        in_specs=[smem] * 4,
        out_specs=smem,
        name="meta",
    )(group, lengths, t_index, slot_target)


def prep(group, slot_target, x):
    clips, _, rows, _ = x.shape
    targets = range(clips)
    ahead = 3

    def kernel(group_ref, slot_ref, x_ref, o_ref, held_ref, in_sems, out_sems):
        base = group_ref[0] * clips
        own = [lax.shift_right_logical(slot_ref[base + i], 3) for i in range(clips)]

        def source(target):
            return sum(jnp.where(own[i] == target, i, 0) for i in range(1, clips))

        sources = [source(target) for target in targets]

        def arriving(n, h):
            columns = x_ref.at[sources[n], :, :, pl.ds(h * HD, HD)]
            return pltpu.make_async_copy(columns, held_ref.at[n, h], in_sems.at[n])

        def all_of(n):
            return pltpu.make_async_copy(held_ref.at[n], held_ref.at[n], in_sems.at[n])

        def leaving(n):
            to = o_ref.at[:, n % CORES, n // CORES]
            return pltpu.make_async_copy(held_ref.at[n], to, out_sems.at[n])

        for n in range(len(targets) + ahead):
            if n < len(targets):
                for h in range(HEADS):
                    arriving(n, h).start()
            if n >= ahead:
                all_of(n - ahead).wait()
                leaving(n - ahead).start()
        for n in range(len(targets)):
            leaving(n).wait()

    smem = pl.BlockSpec(memory_space=pltpu.SMEM)
    anywhere = pl.BlockSpec(memory_space=pl.ANY)
    return pl.pallas_call(
        kernel,
        in_specs=[smem, smem, anywhere],
        out_specs=anywhere,
        out_shape=pltpu.HBM((HEADS, CORES, GROUPS, 3, rows, HD), jnp.bfloat16),
        scratch_shapes=[
            pltpu.VMEM((len(targets), HEADS, 3, rows, HD), jnp.bfloat16),
            pltpu.SemaphoreType.DMA((len(targets),)),
            pltpu.SemaphoreType.DMA((len(targets),)),
        ],
        compiler_params=params(12),
        cost_estimate=cost(0, len(targets) * 12 * rows * HEADS * HD),
        name="prep",
    )(in_hbm(group), in_hbm(slot_target), in_hbm(x))


def spread_kernel(meta_ref, tokens_ref, *out_refs):
    for k in range(CG):

        @pl.when(pl.program_id(0) == k)
        def _(k=k):
            out_refs[k][...] = tokens_ref[0]


def spread(meta, tokens):
    rows, width = tokens.shape[1:]
    return pl.pallas_call(
        spread_kernel,
        grid_spec=pltpu.PrefetchScalarGridSpec(
            num_scalar_prefetch=1,
            grid=(CG,),
            in_specs=[
                pl.BlockSpec((1, rows, width), lambda k, m: (m[SOURCE + m[ORIGIN + k]], 0, 0))
            ],
            out_specs=[pl.BlockSpec((rows, width), lambda k, m: (0, 0))] * CG,
        ),
        out_shape=[pltpu.HBM((rows, width), tokens.dtype)] * CG,
        compiler_params=params(12),
        cost_estimate=cost(0, 4 * math.prod(tokens.shape)),
        name="spread",
    )(meta, in_hbm(tokens))


def rms(part, gain):
    wide = part.astype(jnp.float32)
    mean = jnp.mean(wide * wide, axis=-1, keepdims=True)
    return (wide * lax.rsqrt(mean + 1e-06) * gain).astype(jnp.bfloat16)


def ready(length, tile, tiles, q_gain, k_gain, q_ref, k_ref, v_ref):
    for t in range(tiles):
        to = slice(t * TILE, (t + 1) * TILE)
        q_ref[to] = rms(tile(t, 0), q_gain)
        k_ref[to] = rms(tile(t, 1), k_gain)
        row = t * TILE + lax.broadcasted_iota(jnp.int32, (TILE, HD), 0)
        factor = jnp.where(row < length, 1.0, 0.0).astype(jnp.bfloat16)
        v_ref[to, :HD] = tile(t, 2) * factor
        v_ref[to, HD:] = factor


def attend(n, length, store, q_ref, k_ref, v_ref):
    row = (n - 1) * TILE + lax.broadcasted_iota(jnp.int32, (TILE, HD), 0)
    live = row < length

    def scores_of(t):
        return lax.dot_general(
            q_ref[t * TILE : (t + 1) * TILE],
            k_ref[: n * TILE],
            (((1,), (1,)), ((), ())),
            preferred_element_type=jnp.float32,
        )

    ahead = [scores_of(t) for t in range(min(2, n))]
    for t in range(n):
        scores = ahead.pop(0)
        if t + 2 < n:
            ahead.append(scores_of(t + 2))
        raised = jnp.exp2(scores * SCALE).astype(jnp.bfloat16)
        summed = jnp.dot(raised, v_ref[: n * TILE], preferred_element_type=jnp.float32)
        result = summed[:, :HD] / summed[:, HD:]
        if t == n - 1:
            result = jnp.where(live, result, 0.0)
        store(t, result.astype(jnp.bfloat16))


def attention(meta, y, q_gain, k_gain):
    blocks, cores, groups, parts, rows, _ = y.shape
    total = blocks * rows
    per_tile, tiles = TILE // rows, total // TILE

    clips = cores * groups

    def kernel(meta_ref, y_ref, qg_ref, kg_ref, o_ref, held_ref, sems, *scratch):
        gains = qg_ref[...], kg_ref[...]
        sets = scratch[:3], scratch[3:]

        def arriving(i):
            clip = y_ref.at[:, lax.div(i, groups), lax.rem(i, groups)]
            return pltpu.make_async_copy(clip, held_ref.at[i], sems.at[i])

        for i in range(clips):
            arriving(i).start()

        def tile_of(i):
            def tile(t, part):
                at = slice(t * per_tile, (t + 1) * per_tile)
                return held_ref[i, at, part].reshape(TILE, HD)

            return tile

        def make_ready(i, refs):
            ready(meta_ref[LENGTH + i], tile_of(i), tiles, *gains, *refs)

        def one_clip(i, following, own, other):
            c, x = lax.div(i, groups), lax.rem(i, groups)
            length = meta_ref[LENGTH + i]
            live_tiles = lax.div(length + (TILE - 1), TILE)

            def store(t, result):
                at = slice(t * per_tile, (t + 1) * per_tile)
                o_ref[at, x, c] = result.reshape(per_tile, rows, HD)

            for n in range(1, tiles + 1):

                @pl.when(live_tiles == n)
                def _(n=n):
                    make_ready(following, other)
                    attend(n, length, store, *own)
                    for t in range(n, tiles):
                        store(t, jnp.zeros((TILE, HD), jnp.bfloat16))

        arriving(0).wait()
        make_ready(0, sets[0])

        def two_clips(pair, carry):
            i = 2 * pair
            arriving(i + 1).wait()
            one_clip(i, i + 1, *sets)

            @pl.when(i + 2 < clips)
            def _():
                arriving(i + 2).wait()

            one_clip(i + 1, jnp.minimum(i + 2, clips - 1), *sets[::-1])
            return carry

        lax.fori_loop(0, clips // 2, two_clips, 0)

    vmem = pl.BlockSpec(memory_space=pltpu.VMEM)
    return pl.pallas_call(
        kernel,
        in_specs=[
            pl.BlockSpec(memory_space=pltpu.SMEM),
            pl.BlockSpec(memory_space=pl.ANY),
            vmem,
            vmem,
        ],
        out_specs=vmem,
        out_shape=pltpu.VMEM((blocks, groups, cores, rows, HD), jnp.bfloat16),
        scratch_shapes=[
            pltpu.VMEM((clips, blocks, parts, rows, HD), jnp.bfloat16),
            pltpu.SemaphoreType.DMA((clips,)),
        ]
        + [
            pltpu.VMEM((total, HD), jnp.bfloat16),
            pltpu.VMEM((total, HD), jnp.bfloat16),
            pltpu.VMEM((total, 2 * HD), jnp.bfloat16),
        ]
        * 2,
        compiler_params=params(24),
        cost_estimate=cost(clips * 4 * total * total * HD, clips * total * HD * 8),
        name="attention",
    )(meta, in_hbm(y), q_gain, k_gain)


def load(weight):
    def kernel(from_ref, to_ref, sem):
        copy = pltpu.make_async_copy(from_ref, to_ref, sem)
        copy.start()
        copy.wait()

    return pl.pallas_call(
        kernel,
        in_specs=[pl.BlockSpec(memory_space=pl.ANY)],
        out_specs=pl.BlockSpec(memory_space=pltpu.VMEM),
        out_shape=pltpu.VMEM(weight.shape, weight.dtype),
        scratch_shapes=[pltpu.SemaphoreType.DMA],
        compiler_params=params(16),
        cost_estimate=cost(0, 4 * math.prod(weight.shape)),
        name="load",
    )(in_hbm(weight))


def project(meta, z, weight, gate_table, tokens):
    rows, width = tokens[0].shape
    clips, block = len(tokens), 512
    steps = width // block

    def kernel(meta_ref, z_ref, w_ref, gate_ref, *refs):
        token_refs = refs[:clips]
        out_ref, a_ref, rate_ref, resid_ref, held_ref, in_sems, out_sems = refs[clips:]
        arriving = [
            pltpu.make_async_copy(token_refs[k], resid_ref.at[k], in_sems.at[k])
            for k in range(clips)
        ] + [pltpu.make_async_copy(gate_ref, rate_ref, in_sems.at[clips])]
        for copy in arriving:
            copy.start()
        for k in range(clips):
            origin = meta_ref[ORIGIN + k]
            x, core = lax.shift_right_logical(origin, 1), origin & (CORES - 1)
            for h in range(HEADS):
                a_ref[k * rows : (k + 1) * rows, h * HD : (h + 1) * HD] = z_ref[h, x, core]
        for copy in arriving:
            copy.wait()

        def leaving(n, columns):
            return pltpu.make_async_copy(
                held_ref.at[n], out_ref.at[:, :, columns], out_sems.at[n]
            )

        for n in range(steps):
            columns = pl.ds(n * block, block)
            projected = jnp.dot(a_ref[...], w_ref[:, columns], preferred_element_type=jnp.float32)
            for k in range(clips):
                gate = rate_ref[pl.ds(meta_ref[STEP + k], 1), columns]
                part = gate * projected[k * rows : (k + 1) * rows]
                total = resid_ref[k, :, columns].astype(jnp.float32) + part
                held_ref[n, meta_ref[SLOT + k]] = total.astype(jnp.bfloat16)
            leaving(n, columns).start()
        for n in range(steps):
            leaving(n, pl.ds(n * block, block)).wait()

    smem, vmem, anywhere = (
        pl.BlockSpec(memory_space=space) for space in (pltpu.SMEM, pltpu.VMEM, pl.ANY)
    )
    return pl.pallas_call(
        kernel,
        in_specs=[smem, vmem, vmem, anywhere] + [anywhere] * clips,
        out_specs=anywhere,
        out_shape=pltpu.HBM((clips, rows, width), jnp.bfloat16),
        scratch_shapes=[
            pltpu.VMEM((clips * rows, HEADS * HD), jnp.bfloat16),
            pltpu.VMEM(gate_table.shape, jnp.float32),
            pltpu.VMEM((clips, rows, width), jnp.bfloat16),
            pltpu.VMEM((steps, clips, rows, block), jnp.bfloat16),
            pltpu.SemaphoreType.DMA((clips + 1,)),
            pltpu.SemaphoreType.DMA((steps,)),
        ],
        compiler_params=params(24),
        cost_estimate=cost(
            2 * clips * rows * HEADS * HD * width,
            2 * HEADS * HD * width + 4 * clips * rows * width,
        ),
        name="project",
    )(
        meta,
        in_vmem(z),
        in_vmem(weight),
        in_hbm(gate_table),
        *[in_hbm(part) for part in tokens],
    )


def per_device(qkv, tokens, lengths, t_index, slot_target, gate_table, q_gain, k_gain, out_weight):
    group = lax.axis_index(("x", "core"))
    group = group.reshape(1)
    meta = make_meta(group, lengths, t_index, slot_target)

    def across(part, k):
        pairs = [(g, g ^ k) for g in range(CG)]
        return lax.ppermute(part, ("x", "core"), pairs) if k else part

    def exchange(array, axes, kept):
        sent = array.reshape(-1, *array.shape[kept:])
        arrived = lax.all_to_all(sent, axes, split_axis=0, concat_axis=0, tiled=True)
        return arrived.reshape(array.shape)

    resid = [across(part, k) for k, part in enumerate(spread(meta, tokens))]
    weight = load(out_weight)
    y = exchange(prep(group, slot_target, jnp.swapaxes(qkv, 1, 2)), ("z", "y", "core"), 2)
    y, weight, *resid = lax.optimization_barrier((y, weight, *resid))
    attended = attention(meta, y, q_gain.reshape(1, HD), k_gain.reshape(1, HD))
    z = exchange(attended, ("z", "y", "x"), 2)
    return project(meta, z, weight, gate_table, resid)


def solution(mesh):
    apart = Mesh(mesh.devices.reshape(GROUPS, CORES, 4, 4), ("x", "core", "z", "y"))
    clips, tokens = ("x", "core"), ("z", "y")
    return jax.shard_map(
        per_device,
        mesh=apart,
        in_specs=(
            P(clips, tokens, None, None),
            P(clips, tokens, None),
            P(),
            P(),
            P(),
            P(),
            P(),
            P(),
            P(),
        ),
        out_specs=P(clips, tokens, None),
        check_vma=False,
    )
```
